256 devices in a mesh: dp: 2 (over x_lo), ctx: 16 (over z, x_hi), tp: 8 (over y, core).
Axes of the slice: x: 4 (x_hi: 2, x_lo: 2; x = x_hi * 2 + x_lo), y: 4, z: 8, core: 2. Of those that a mesh axis runs over, the one named last changes fastest.
Arguments:
- queries: bfloat16 [2, 8192, 8192], P('dp', ('ctx', 'tp')), may hold values from -300 to 300
- key_rows: bfloat16 [2, 8192, 1024], P('dp', ('ctx', 'tp')), may hold values from -12 to 12
- values_in: bfloat16 [2, 8192, 1024], P('dp', ('ctx', 'tp')), may hold values from -6 to 6
- out_grad: bfloat16 [2, 8192, 8192], P('dp', ('ctx', 'tp')), may hold values from -6 to 6
- send_rows: int32 [2, 128, 64], P('dp', ('ctx', 'tp')), may hold values from 0 to 63, each once within a row
- doc_lengths: int32 [2, 32], P('dp'), may hold values from 1 to 1024, 8192 in all within a row
Outputs:
- attended: bfloat16 [2, 8192, 8192], P('dp', 'ctx', 'tp')
- query_grad: bfloat16 [2, 8192, 8192], P('dp', 'ctx', 'tp')
- key_grad: bfloat16 [2, 8192, 1024], P('dp', 'ctx', 'tp')
- value_grad: bfloat16 [2, 8192, 1024], P('dp', 'ctx', 'tp')
The draws below stay inside these ranges and needn't reach their ends.
Inputs may be any that keep to these rules, and one draw needn't show every extreme that they name: Each row send_rows[d, b] is a permutation of the 64 rows that old replica d holds in slot b; its entries e * 32 to (e + 1) * 32 - 1 name the rows that move to replica e. `doc_lengths`: each row sums to 8192; its longest document has exactly 1024 positions.
All inputs are finite; a program needn't handle non-finite values.
Results may differ from the reference program's by a relative error of at most 0.015.
Values may be sent and summed in bfloat16 or wider, within the bound.
No kernel may reach another device: no remote copies, remote signals or barrier semaphores. Data moves between devices by JAX's collectives and lax.ppermute only.
A program may use at most 64 MiB of HBM per device.

```python
import math
import jax
import jax.numpy as jnp
import numpy as np
from jax import lax

QH = 64
KVH = 8
HD = 128
TOK_DEV = 512
SPAN = 2
GROUP = 8
SEQ = 8192
ROWS = 64
MAXDOC = 1024
NDOCS = 32
N_DP = 2
N_CTX = 16
N_TP = 8


def common_keys(key):
    return jax.random.normal(key, (N_DP, SEQ, KVH * HD), jnp.float32)


def draw_key_rows(key, part):
    base = common_keys(key)
    return base.astype(jnp.bfloat16)


def draw_queries(key, part):
    key = jax.random.fold_in(key, 7)
    fresh = jax.random.normal(key, (N_DP, SEQ, QH * HD), jnp.float32)
    return fresh.astype(jnp.bfloat16)


def levels(key, dims, pieces, low, top_value):
    gain = 1.0
    for position, blocks in pieces:
        steps = jax.random.uniform(jax.random.fold_in(jax.random.fold_in(key, 6), position), (blocks,), jnp.float32, low / len(pieces), top_value / len(pieces))
        gain = gain * jnp.repeat(jnp.exp(steps), dims[position] // blocks).reshape((-1,) + (1,) * (len(dims) - 1 - position))
    return gain


def split_up(number_of, total, reach, slope):
    weights = [(1 << 20) // math.isqrt(standing ** slope) + 1 for standing in range(2, number_of + 1)]
    spare, counts = total - reach - (number_of - 1), [1] * (number_of - 1)
    while spare > 0:
        candidates = [i for i in range(number_of - 1) if counts[i] < reach]
        pool, budget = sum([weights[i] for i in candidates]), spare
        for i in candidates:
            more = min(reach - counts[i], max(1, budget * weights[i] // pool), spare)
            counts[i] = counts[i] + more
            spare = spare - more
    return np.array([reach] + counts)


def uneven(own_key, amount, total, reach, slope):
    if amount == 2:
        one = jax.random.randint(own_key, (), max(1, total - reach), min(reach, total - 1) + 1)
        return jnp.stack([one, total - one])
    sizes = jnp.asarray(split_up(amount, total, reach, slope), jnp.int32)
    twos = (amount - 1) // 2
    giver, sink = sizes[1:1 + 2 * twos:2], sizes[2:2 + 2 * twos:2]
    room = jnp.minimum(giver - 1, reach - sink)
    passed = jax.random.randint(jax.random.fold_in(own_key, 1), (twos,), 0, 1 << 20) % (room + 1)
    sizes = sizes.at[1:1 + 2 * twos:2].set(giver - passed).at[2:2 + 2 * twos:2].set(sink + passed)
    return sizes[jax.random.permutation(jax.random.fold_in(own_key, 2), amount)]


def centred(stream_key, dims, scale, reach, cuts=(), kind=jnp.bfloat16):
    drawn = scale * jax.random.normal(stream_key, dims, jnp.float32)
    if cuts:
        drawn = drawn * levels(stream_key, dims, cuts, -0.22, 0.18)
    return jnp.clip(drawn, -reach, reach).astype(kind)


def setup_inputs(seed: int = 0) -> dict:
    key_of = jax.random.split(jax.random.key(seed), 7)
    return {
        "queries": draw_queries(jax.random.fold_in(key_of[6], 71), 0),
        "key_rows": draw_key_rows(jax.random.fold_in(key_of[6], 71), 0),
        "values_in": centred(key_of[2], (N_DP, SEQ, KVH * HD), 1.0, 6.0, ((0, 2), (1, 128))),
        "out_grad": centred(key_of[3], (N_DP, SEQ, QH * HD), 1.0, 6.0, ((0, 2), (1, 128))),
        "send_rows": jax.vmap(lambda own: jax.random.permutation(own, ROWS))(jax.random.split(key_of[4], N_DP * (N_CTX * N_TP))).reshape((N_DP, N_CTX * N_TP, ROWS)).astype(jnp.int32),
        "doc_lengths": jax.vmap(lambda own: uneven(own, NDOCS, SEQ, MAXDOC, 2))(jax.random.split(key_of[5], N_DP)).reshape((N_DP, NDOCS)).astype(jnp.int32),
    }


def regroup(array, send_rows):
    width = array.shape[2]
    slots = N_CTX * N_TP
    flat = array.reshape(N_DP * SEQ, width)
    base = (jnp.arange(N_DP * slots, dtype=jnp.int32) * ROWS).reshape(N_DP, slots, 1)
    index = (base + send_rows).reshape(-1)
    picked = jnp.take(flat, index, axis=0)
    picked = picked.reshape(N_DP, N_CTX, N_TP, N_DP, ROWS // N_DP, width)
    moved = picked.transpose(3, 1, 2, 0, 4, 5)
    return moved.reshape(N_DP, SEQ, width)

def segment_ids(starts, positions):
    return lax.optimization_barrier(jnp.sum((starts[None, :] <= positions[:, None]).astype(jnp.int32), axis=1)) - 1

def attend(query_block, key_win, value_win, grad_block, allowed):
    scale = 1.0 / math.sqrt(HD)
    scores = jnp.einsum('qgd,kd->gqk', query_block.astype(jnp.float32), key_win.astype(jnp.float32)) * scale
    scores = jnp.where(allowed[None], scores, -1e+30)
    top = lax.optimization_barrier(jnp.max(scores, axis=-1, keepdims=True))
    expo = jnp.exp(scores - top)
    prob = (expo / lax.optimization_barrier(jnp.sum(expo, axis=-1, keepdims=True))).astype(jnp.bfloat16)
    output = jnp.einsum('gqk,kd->qgd', prob.astype(jnp.float32), value_win.astype(jnp.float32)).astype(jnp.bfloat16)
    delta = lax.optimization_barrier(jnp.sum(grad_block.astype(jnp.float32) * output.astype(jnp.float32), axis=-1))
    dprob = jnp.einsum('qgd,kd->gqk', grad_block.astype(jnp.float32), value_win.astype(jnp.float32))
    dscore = (prob.astype(jnp.float32) * (dprob - delta.T[:, :, None]) * scale).astype(jnp.bfloat16)
    dquery = jnp.einsum('gqk,kd->qgd', dscore.astype(jnp.float32), key_win.astype(jnp.float32)).astype(jnp.bfloat16)
    dkey = jnp.einsum('gqk,qgd->kd', dscore.astype(jnp.float32), query_block.astype(jnp.float32))
    dvalue = jnp.einsum('gqk,qgd->kd', prob.astype(jnp.float32), grad_block.astype(jnp.float32))
    return (output, dquery, dkey, dvalue)

def replica(query_seq, key_seq, value_seq, grad_seq, lengths):
    starts = jnp.cumsum(lengths) - lengths
    segments = segment_ids(starts, jnp.arange(SEQ, dtype=jnp.int32))
    margin = SPAN * TOK_DEV
    width = (SPAN + 1) * TOK_DEV
    key_pad = jnp.concatenate([jnp.zeros((margin, KVH * HD), key_seq.dtype), key_seq], axis=0)
    value_pad = jnp.concatenate([jnp.zeros((margin, KVH * HD), value_seq.dtype), value_seq], axis=0)
    seg_pad = jnp.concatenate([jnp.full((margin,), -1, jnp.int32), segments], axis=0)
    query_four = query_seq.reshape(SEQ, KVH, GROUP, HD)
    grad_four = grad_seq.reshape(SEQ, KVH, GROUP, HD)

    def block_step(carry, block):
        dkey_pad, dvalue_pad = carry
        first = (block * TOK_DEV).astype(jnp.int32)
        query_block = lax.dynamic_slice_in_dim(query_four, first, TOK_DEV, 0)
        grad_block = lax.dynamic_slice_in_dim(grad_four, first, TOK_DEV, 0)
        key_win = lax.dynamic_slice_in_dim(key_pad, first, width, 0).reshape(width, KVH, HD)
        value_win = lax.dynamic_slice_in_dim(value_pad, first, width, 0).reshape(width, KVH, HD)
        query_seg = lax.dynamic_slice_in_dim(segments, first, TOK_DEV, 0)
        key_seg = lax.dynamic_slice_in_dim(seg_pad, first, width, 0)
        query_pos = first + jnp.arange(TOK_DEV, dtype=jnp.int32)
        key_pos = first - margin + jnp.arange(width, dtype=jnp.int32)
        allowed = (key_pos[None, :] <= query_pos[:, None]) & (key_seg[None, :] == query_seg[:, None])

        def per_head(head):
            return attend(query_block[:, head], key_win[:, head], value_win[:, head], grad_block[:, head], allowed)
        output, dquery, dkey, dvalue = lax.map(per_head, jnp.arange(KVH, dtype=jnp.int32))
        dkey = dkey.transpose(1, 0, 2).reshape(width, KVH * HD)
        dvalue = dvalue.transpose(1, 0, 2).reshape(width, KVH * HD)
        dkey_pad = lax.dynamic_update_slice_in_dim(dkey_pad, lax.dynamic_slice_in_dim(dkey_pad, first, width, 0) + dkey, first, 0)
        dvalue_pad = lax.dynamic_update_slice_in_dim(dvalue_pad, lax.dynamic_slice_in_dim(dvalue_pad, first, width, 0) + dvalue, first, 0)
        output = output.transpose(1, 0, 2, 3).reshape(TOK_DEV, QH * HD)
        dquery = dquery.transpose(1, 0, 2, 3).reshape(TOK_DEV, QH * HD)
        return ((dkey_pad, dvalue_pad), (output, dquery))
    start_carry = (jnp.zeros((margin + SEQ, KVH * HD), jnp.float32), jnp.zeros((margin + SEQ, KVH * HD), jnp.float32))
    (dkey_pad, dvalue_pad), (output, dquery) = lax.scan(block_step, start_carry, jnp.arange(N_CTX, dtype=jnp.int32))
    return (output.reshape(SEQ, QH * HD), dquery.reshape(SEQ, QH * HD), dkey_pad[margin:].astype(jnp.bfloat16), dvalue_pad[margin:].astype(jnp.bfloat16))

def reference(queries, key_rows, values_in, out_grad, send_rows, doc_lengths):
    query_new = regroup(queries, send_rows)
    key_new = regroup(key_rows, send_rows)
    value_new = regroup(values_in, send_rows)
    grad_new = regroup(out_grad, send_rows)
    results = [replica(query_new[index], key_new[index], value_new[index], grad_new[index], doc_lengths[index]) for index in range(N_DP)]
    attended = jnp.stack([item[0] for item in results])
    query_grad = jnp.stack([item[1] for item in results])
    key_grad = jnp.stack([item[2] for item in results])
    value_grad = jnp.stack([item[3] for item in results])
    return (attended, query_grad, key_grad, value_grad)
```

```python
import functools
import math

import jax
import jax.numpy as jnp
from jax import lax
from jax.experimental import pallas as pl
from jax.experimental.pallas import tpu as pltpu
from jax.sharding import PartitionSpec as P

HD = 128
SPAN = 2
FIRST_HEADS = 4
STEP_HEADS = 2
TILE = 256
SCALE = 1.0 / math.sqrt(HD)
LOG2_SCALE = math.log2(math.e) * SCALE
NT = (((1,), (1,)), ((), ()))
NN = (((1,), (0,)), ((), ()))
TN = (((0,), (0,)), ((), ()))


def dot(a, b, dims):
    return lax.dot_general(a, b, dims, preferred_element_type=jnp.float32)


def pack_kernel(heads, first, order_ref, q_ref, k_ref, v_ref, g_ref, one_ref, two_ref):
    rows = q_ref.shape[0]
    group = rows // one_ref.shape[0]
    row = lax.broadcasted_iota(jnp.int32, (rows, rows), 0)
    pick = (row == order_ref[...]).astype(jnp.bfloat16)
    cut = first * HD

    def put(ref, begin, block):
        moved = dot(pick, block, TN).astype(jnp.bfloat16)
        for replica in range(ref.shape[0]):
            ref[replica, :, begin : begin + block.shape[1]] = moved[
                replica * group : (replica + 1) * group
            ]

    put(one_ref, 0, k_ref[...])
    put(one_ref, HD, v_ref[...])
    put(one_ref, 2 * HD, q_ref[:, :cut])
    put(one_ref, 2 * HD + cut, g_ref[:, :cut])
    put(two_ref, 0, q_ref[:, cut:])
    put(two_ref, heads * HD - cut, g_ref[:, cut:])


def pack(order, queries, key_rows, values_in, out_grad, replicas, slots, first):
    rows = queries.shape[0]
    heads = queries.shape[1] // slots // HD
    wide = pl.BlockSpec((rows, heads * HD), lambda t: (0, t))
    thin = pl.BlockSpec((rows, HD), lambda t: (0, t))
    widths = (2 * HD + 2 * first * HD, 2 * (heads - first) * HD)
    return pl.pallas_call(
        functools.partial(pack_kernel, heads, first),
        grid=(slots,),
        in_specs=[pl.BlockSpec((1, rows), lambda t: (0, 0)), wide, thin, thin, wide],
        out_specs=[
            pl.BlockSpec((replicas, rows // replicas, w), lambda t: (t, 0, 0)) for w in widths
        ],
        out_shape=[
            jax.ShapeDtypeStruct((slots * replicas, rows // replicas, w), jnp.bfloat16)
            for w in widths
        ],
        compiler_params=pltpu.CompilerParams(vmem_limit_bytes=32 * 2**20),
    )(order, queries, key_rows, values_in, out_grad)


def fill_bias(lengths_ref, bias_ref):
    block_rows = bias_ref.shape[0]
    margin = SPAN * block_rows
    docs = lengths_ref.shape[1]
    lengths = lengths_ref[...].astype(jnp.float32)
    down = lax.broadcasted_iota(jnp.int32, (docs, docs), 0)
    across = lax.broadcasted_iota(jnp.int32, (docs, docs), 1)
    column = jnp.sum(jnp.where(down == across, lengths, 0.0), axis=1, keepdims=True)
    starts = jnp.sum(jnp.where(down < across, column, 0.0), axis=0, keepdims=True)
    first = lax.axis_index("ctx") * block_rows
    place = first + lax.broadcasted_iota(jnp.int32, (block_rows, docs), 0)
    begun = starts <= place.astype(jnp.float32)
    begin = jnp.max(jnp.where(begun, starts, 0.0), axis=1, keepdims=True).astype(jnp.int32)
    begin = begin - (first - margin)
    for t in range(block_rows // TILE):
        here = slice(t * TILE, (t + 1) * TILE)
        row = lax.broadcasted_iota(jnp.int32, (TILE, margin + TILE), 0)
        col = lax.broadcasted_iota(jnp.int32, (TILE, margin + TILE), 1)
        allowed = (col <= row + margin) & (col >= begin[here] - t * TILE)
        bias_ref[here, :] = jnp.where(allowed, 0.0, -1e30)


def one_head(cols, q_ref, g_ref, key_win, value_win, bias_ref, out_ref, dq_ref, dk_ref, dv_ref):
    block_rows = q_ref.shape[0]
    margin = SPAN * block_rows
    for t in range(block_rows // TILE):
        here = slice(t * TILE, (t + 1) * TILE)
        window = slice(t * TILE, (t + 1) * TILE + margin)
        query, grad = q_ref[here, cols], g_ref[here, cols]
        key, value = key_win[window, :], value_win[window, :]
        scores = dot(query, key, NT) * LOG2_SCALE + bias_ref[here, :]
        top = jnp.max(scores, axis=1, keepdims=True)
        expo = jnp.exp2(scores - top)
        inverse = 1.0 / jnp.sum(expo, axis=1, keepdims=True)
        prob = expo.astype(jnp.bfloat16)
        output = (dot(prob, value, NN) * inverse).astype(jnp.bfloat16)
        out_ref[here, cols] = output
        grad = (grad.astype(jnp.float32) * inverse).astype(jnp.bfloat16)
        delta = jnp.sum(
            grad.astype(jnp.float32) * output.astype(jnp.float32), axis=1, keepdims=True
        )
        dprob = dot(grad, value, NT)
        dscore = (prob.astype(jnp.float32) * (dprob - delta)).astype(jnp.bfloat16)
        dq_ref[here, cols] = (dot(dscore, key, NN) * SCALE).astype(jnp.bfloat16)
        dv_ref[:, window] += dot(grad, prob, TN)
        dk_ref[:, window] += dot(query, dscore, TN)


def gather_window(k_ref, v_ref, kv1_ref, kv2_ref, key_win, value_win):
    block_rows = k_ref.shape[0]
    for place, ref in ((0, kv2_ref), (1, kv1_ref)):
        here = slice(place * block_rows, (place + 1) * block_rows)
        key_win[here, :] = ref[:, :HD]
        value_win[here, :] = ref[:, HD:]
    key_win[SPAN * block_rows :, :] = k_ref[...]
    value_win[SPAN * block_rows :, :] = v_ref[...]


def first_kernel(
    lengths_ref, q_ref, g_ref, k_ref, v_ref, kv1_ref, kv2_ref,
    out_ref, dq_ref, dk_ref, dv_ref,
    key_win, value_win, bias_ref,
):
    @pl.when(pl.program_id(0) == 0)
    def _():
        gather_window(k_ref, v_ref, kv1_ref, kv2_ref, key_win, value_win)
        fill_bias(lengths_ref, bias_ref)
        dk_ref[...] = jnp.zeros_like(dk_ref)
        dv_ref[...] = jnp.zeros_like(dv_ref)

    for head in range(STEP_HEADS):
        one_head(
            slice(head * HD, (head + 1) * HD),
            q_ref, g_ref, key_win, value_win, bias_ref, out_ref, dq_ref, dk_ref, dv_ref,
        )


def second_kernel(
    lengths_ref, q_ref, g_ref, k_ref, v_ref, kv1_ref, kv2_ref, dk_in, dv_in, out_in, dq_in,
    out_ref, dq_ref, own_ref, back1_ref, back2_ref,
    key_win, value_win, bias_ref, dk_ref, dv_ref,
):
    @pl.when(pl.program_id(0) == 0)
    def _():
        gather_window(k_ref, v_ref, kv1_ref, kv2_ref, key_win, value_win)
        fill_bias(lengths_ref, bias_ref)
        dk_ref[...] = dk_in[...]
        dv_ref[...] = dv_in[...]

    for head in range(STEP_HEADS):
        one_head(
            slice(head * HD, (head + 1) * HD),
            q_ref, g_ref, key_win, value_win, bias_ref, out_ref, dq_ref, dk_ref, dv_ref,
        )

    @pl.when(pl.program_id(0) == pl.num_programs(0) - 1)
    def _():
        block_rows = q_ref.shape[0]
        for place, ref in ((0, back2_ref), (1, back1_ref), (2, own_ref)):
            here = slice(place * block_rows, (place + 1) * block_rows)
            ref[:, :HD] = (dk_ref[:, here] * SCALE).T.astype(ref.dtype)
            ref[:, HD:] = dv_ref[:, here].T.astype(ref.dtype)


def attend(one, two, back1, back2, lengths, heads, first):
    block_rows = one.shape[0]
    width = (SPAN + 1) * block_rows
    step = STEP_HEADS * HD
    whole = lambda shape: pl.BlockSpec(shape, lambda h: (0, 0))
    columns = lambda begin: pl.BlockSpec((block_rows, step), lambda h: (0, begin + h))
    key_part = pl.BlockSpec((block_rows, HD), lambda h: (0, 0))
    value_part = pl.BlockSpec((block_rows, HD), lambda h: (0, 1))
    pair = (block_rows, 2 * HD)
    out = jax.ShapeDtypeStruct((block_rows, heads * HD), jnp.bfloat16)
    total = jax.ShapeDtypeStruct((HD, width), jnp.float32)
    params = pltpu.CompilerParams(vmem_limit_bytes=40 * 2**20)
    window = [
        pltpu.VMEM((width, HD), jnp.bfloat16),
        pltpu.VMEM((width, HD), jnp.bfloat16),
        pltpu.VMEM((block_rows, SPAN * block_rows + TILE), jnp.float32),
    ]
    lead = 2 * HD // step
    attended, query_grad, dk, dv = pl.pallas_call(
        first_kernel,
        grid=(first // STEP_HEADS,),
        in_specs=[
            whole(lengths.shape),
            columns(lead), columns(lead + first // STEP_HEADS),
            key_part, value_part, whole(pair), whole(pair),
        ],
        out_specs=[columns(0), columns(0), whole(total.shape), whole(total.shape)],
        out_shape=[out, out, total, total],
        scratch_shapes=window,
        compiler_params=params,
    )(lengths, one, one, one, one, back1, back2)
    rest = heads - first
    begin = first // STEP_HEADS
    return pl.pallas_call(
        second_kernel,
        grid=(rest // STEP_HEADS,),
        in_specs=[
            whole(lengths.shape),
            columns(0), columns(rest // STEP_HEADS),
            key_part, value_part, whole(pair), whole(pair),
            whole(total.shape), whole(total.shape),
            pl.BlockSpec(memory_space=pl.ANY), pl.BlockSpec(memory_space=pl.ANY),
        ],
        out_specs=[columns(begin), columns(begin), whole(pair), whole(pair), whole(pair)],
        out_shape=[
            out, out,
            jax.ShapeDtypeStruct(pair, jnp.float32),
            jax.ShapeDtypeStruct(pair, jnp.bfloat16),
            jax.ShapeDtypeStruct(pair, jnp.bfloat16),
        ],
        scratch_shapes=window + [
            pltpu.VMEM(total.shape, jnp.float32), pltpu.VMEM(total.shape, jnp.float32)
        ],
        input_output_aliases={9: 0, 10: 1},
        compiler_params=params,
    )(lengths, two, two, one, one, back1, back2, dk, dv, attended, query_grad)


def shifted(block, axis, distance):
    devices = range(lax.axis_size(axis))
    route = [(i - distance, i) for i in devices if i - distance in devices]
    return lax.ppermute(block, axis, route)


def exchange(block):
    return lax.all_to_all(block, ("tp", "dp"), split_axis=0, concat_axis=0, tiled=True)


def on_device(queries, key_rows, values_in, out_grad, send_rows, doc_lengths):
    replicas, slots = lax.axis_size("dp"), lax.axis_size("tp")
    heads = queries.shape[2] // slots // HD
    one, two = pack(
        send_rows[0], queries[0], key_rows[0], values_in[0], out_grad[0], replicas, slots, FIRST_HEADS
    )
    one = exchange(one)
    one = one.reshape(one.shape[0] * one.shape[1], one.shape[2])
    key_value = one[:, : 2 * HD]
    previous = [shifted(key_value, "ctx", offset) for offset in range(1, SPAN + 1)]
    two = exchange(two)
    two = two.reshape(two.shape[0] * two.shape[1], two.shape[2])
    attended, query_grad, own, back1, back2 = attend(
        one, two, previous[0], previous[1], doc_lengths, heads, FIRST_HEADS
    )
    for offset, part in ((2, back2), (1, back1)):
        own = own + shifted(part, "ctx", -offset).astype(jnp.float32)
    own = own.astype(jnp.bfloat16)
    return (attended[None], query_grad[None], own[None, :, :HD], own[None, :, HD:])


def solution(mesh):
    rows = P("dp", ("ctx", "tp"), None)
    out = P("dp", "ctx", "tp")
    return jax.shard_map(
        on_device,
        mesh=mesh,
        in_specs=(rows, rows, rows, rows, rows, P("dp", None)),
        out_specs=(out, out, out, out),
        check_vma=False,
    )
```

```python
import functools
import math

import jax
import jax.numpy as jnp
from jax import lax
from jax.experimental import pallas as pl
from jax.experimental.pallas import tpu as pltpu
from jax.sharding import PartitionSpec as P

HD = 128
SPAN = 2
FIRST_HEADS = 5
PACK_SLOTS = 2
TILE = 256
SCALE = 1.0 / math.sqrt(HD)
LOG2_SCALE = math.log2(math.e) * SCALE
NT = (((1,), (1,)), ((), ()))
NN = (((1,), (0,)), ((), ()))
TN = (((0,), (0,)), ((), ()))


def dot(a, b, dims):
    return lax.dot_general(a, b, dims, preferred_element_type=jnp.float32)


def select(order_ref):
    rows = order_ref.shape[1]
    row = lax.broadcasted_iota(jnp.int32, (rows, rows), 0)
    return (row == order_ref[...]).astype(jnp.bfloat16)


def put(ref, slot, begin, moved):
    group = ref.shape[1]
    replicas = moved.shape[0] // group
    for replica in range(replicas):
        ref[slot * replicas + replica, :, begin : begin + moved.shape[1]] = moved[
            replica * group : (replica + 1) * group
        ]


def pack_small_kernel(order_ref, k_ref, v_ref, sent_ref):
    pick = select(order_ref)
    for begin, ref in ((0, k_ref), (HD, v_ref)):
        moved = dot(pick, ref[...], TN).astype(jnp.bfloat16)
        for slot in range(moved.shape[1] // HD):
            put(sent_ref, slot, begin, moved[:, slot * HD : (slot + 1) * HD])


def pack_large_kernel(heads, first, order_ref, q_ref, g_ref, one_ref, two_ref):
    pick = select(order_ref)
    cut = first * HD
    for index, ref in enumerate((q_ref, g_ref)):
        for slot in range(ref.shape[1] // (heads * HD)):
            begin = slot * heads * HD
            moved = dot(pick, ref[:, begin : begin + heads * HD], TN).astype(jnp.bfloat16)
            put(one_ref, slot, index * cut, moved[:, :cut])
            put(two_ref, slot, index * (heads * HD - cut), moved[:, cut:])


def in_hbm(*arrays):
    return [pltpu.with_memory_space_constraint(a, pltpu.HBM) for a in arrays]


def pack_small(order, key_rows, values_in, replicas, slots):
    rows, columns = key_rows.shape
    whole = lambda shape: pl.BlockSpec(shape, lambda: (0,) * len(shape))
    sent = (slots * replicas, rows // replicas, 2 * columns // slots)
    return pl.pallas_call(
        pack_small_kernel,
        in_specs=[whole(order.shape), whole(key_rows.shape), whole(values_in.shape)],
        out_specs=whole(sent),
        out_shape=jax.ShapeDtypeStruct(sent, jnp.bfloat16),
        compiler_params=pltpu.CompilerParams(vmem_limit_bytes=16 * 2**20),
    )(*in_hbm(order, key_rows, values_in))


def pack_large(order, queries, out_grad, replicas, slots, first):
    rows, columns = queries.shape
    heads = columns // slots // HD
    wide = pl.BlockSpec((rows, PACK_SLOTS * heads * HD), lambda t: (0, t))
    widths = (2 * first * HD, 2 * (heads - first) * HD)
    return pl.pallas_call(
        functools.partial(pack_large_kernel, heads, first),
        grid=(slots // PACK_SLOTS,),
        in_specs=[pl.BlockSpec(order.shape, lambda t: (0, 0)), wide, wide],
        out_specs=[
            pl.BlockSpec((PACK_SLOTS * replicas, rows // replicas, w), lambda t: (t, 0, 0))
            for w in widths
        ],
        out_shape=[
            jax.ShapeDtypeStruct((slots * replicas, rows // replicas, w), jnp.bfloat16)
            for w in widths
        ],
        compiler_params=pltpu.CompilerParams(vmem_limit_bytes=32 * 2**20),
    )(*in_hbm(order, queries, out_grad))


def fill_bias(lengths_ref, bias_ref):
    block_rows = bias_ref.shape[0]
    margin = SPAN * block_rows
    docs = lengths_ref.shape[1]
    lengths = lengths_ref[...].astype(jnp.float32)
    down = lax.broadcasted_iota(jnp.int32, (docs, docs), 0)
    across = lax.broadcasted_iota(jnp.int32, (docs, docs), 1)
    column = jnp.sum(jnp.where(down == across, lengths, 0.0), axis=1, keepdims=True)
    starts = jnp.sum(jnp.where(down < across, column, 0.0), axis=0, keepdims=True)
    first = lax.axis_index("ctx") * block_rows
    place = first + lax.broadcasted_iota(jnp.int32, (block_rows, docs), 0)
    begun = starts <= place.astype(jnp.float32)
    begin = jnp.max(jnp.where(begun, starts, 0.0), axis=1, keepdims=True).astype(jnp.int32)
    begin = begin - (first - margin)
    for t in range(block_rows // TILE):
        here = slice(t * TILE, (t + 1) * TILE)
        row = lax.broadcasted_iota(jnp.int32, (TILE, margin + TILE), 0)
        col = lax.broadcasted_iota(jnp.int32, (TILE, margin + TILE), 1)
        allowed = (col <= row + margin) & (col >= begin[here] - t * TILE)
        bias_ref[here, :] = jnp.where(allowed, 0.0, -1e30)


def stacked(ref, here, begin, heads):
    return jnp.concatenate(
        [ref[here, begin + h * HD : begin + (h + 1) * HD] for h in range(heads)], axis=0
    )


def heads_pass(
    heads, column, rows_ref, key_win, value_win, bias_ref, dk_ref, dv_ref,
    out_stage, dq_stage, out_hbm, dq_hbm, sems,
):
    block_rows = rows_ref.shape[0]
    margin = SPAN * block_rows
    width = margin + TILE
    copies = []
    for t in range(block_rows // TILE):
        here = slice(t * TILE, (t + 1) * TILE)
        window = slice(t * TILE, t * TILE + width)
        query = stacked(rows_ref, here, 0, heads)
        grad = stacked(rows_ref, here, heads * HD, heads)
        key, value = key_win[window, :], value_win[window, :]
        scores = (dot(query, key, NT) * LOG2_SCALE).reshape(heads, TILE, width)
        scores = (scores + bias_ref[here, :][None]).reshape(heads * TILE, width)
        top = jnp.max(scores, axis=1, keepdims=True)
        expo = jnp.exp2(scores - top)
        inverse = 1.0 / jnp.sum(expo, axis=1, keepdims=True)
        prob = expo.astype(jnp.bfloat16)
        output = (dot(prob, value, NN) * inverse).astype(jnp.bfloat16)
        grad = (grad.astype(jnp.float32) * inverse).astype(jnp.bfloat16)
        delta = jnp.sum(
            grad.astype(jnp.float32) * output.astype(jnp.float32), axis=1, keepdims=True
        )
        dprob = dot(grad, value, NT)
        dscore = (prob.astype(jnp.float32) * (dprob - delta)).astype(jnp.bfloat16)
        dquery = (dot(dscore, key, NN) * SCALE).astype(jnp.bfloat16)
        for h in range(heads):
            cols = slice(h * HD, (h + 1) * HD)
            out_stage[here, cols] = output[h * TILE : (h + 1) * TILE]
            dq_stage[here, cols] = dquery[h * TILE : (h + 1) * TILE]
        for which, (stage, target) in enumerate(((out_stage, out_hbm), (dq_stage, dq_hbm))):
            copies.append(
                pltpu.make_async_copy(
                    stage.at[here, :],
                    target.at[here, column * HD : (column + heads) * HD],
                    sems.at[2 * t + which],
                )
            )
            copies[-1].start()
        dv_ref[:, window] += dot(grad, prob, TN)
        dk_ref[:, window] += dot(query, dscore, TN)
    return copies


def gather_window(kv_ref, kv1_ref, kv2_ref, key_win, value_win):
    block_rows = kv_ref.shape[0]
    for place, ref in ((0, kv2_ref), (1, kv1_ref), (2, kv_ref)):
        here = slice(place * block_rows, (place + 1) * block_rows)
        key_win[here, :] = ref[:, :HD]
        value_win[here, :] = ref[:, HD:]


def first_kernel(
    heads, lengths_ref, rows_ref, kv_ref, kv1_ref, kv2_ref,
    out_hbm, dq_hbm, dk_ref, dv_ref,
    key_win, value_win, bias_ref, out_stage, dq_stage, sems,
):
    gather_window(kv_ref, kv1_ref, kv2_ref, key_win, value_win)
    fill_bias(lengths_ref, bias_ref)
    dk_ref[...] = jnp.zeros_like(dk_ref)
    dv_ref[...] = jnp.zeros_like(dv_ref)
    copies = heads_pass(
        heads, 0, rows_ref, key_win, value_win, bias_ref, dk_ref, dv_ref,
        out_stage, dq_stage, out_hbm, dq_hbm, sems,
    )
    for copy in copies:
        copy.wait()


def second_kernel(
    heads, column, lengths_ref, rows_ref, kv_ref, kv1_ref, kv2_ref, dk_in, dv_in, out_in, dq_in,
    out_hbm, dq_hbm, own_ref, back1_ref, back2_ref,
    key_win, value_win, bias_ref, out_stage, dq_stage, sems, dk_ref, dv_ref,
):
    gather_window(kv_ref, kv1_ref, kv2_ref, key_win, value_win)
    fill_bias(lengths_ref, bias_ref)
    dk_ref[...] = dk_in[...]
    dv_ref[...] = dv_in[...]
    copies = heads_pass(
        heads, column, rows_ref, key_win, value_win, bias_ref, dk_ref, dv_ref,
        out_stage, dq_stage, out_hbm, dq_hbm, sems,
    )
    block_rows = rows_ref.shape[0]
    for place, ref in ((0, back2_ref), (1, back1_ref), (2, own_ref)):
        here = slice(place * block_rows, (place + 1) * block_rows)
        ref[:, :HD] = (dk_ref[:, here] * SCALE).T.astype(ref.dtype)
        ref[:, HD:] = dv_ref[:, here].T.astype(ref.dtype)
    for copy in copies:
        copy.wait()


def attend(one, two, key_value, back1, back2, lengths, heads, first):
    block_rows = one.shape[0]
    width = (SPAN + 1) * block_rows
    whole = lambda shape: pl.BlockSpec(shape, lambda: (0, 0))
    anywhere = pl.BlockSpec(memory_space=pl.ANY)
    pair = key_value.shape
    out = pltpu.HBM((block_rows, heads * HD), jnp.bfloat16)
    total = (HD, width)
    params = pltpu.CompilerParams(vmem_limit_bytes=44 * 2**20)
    inputs = [whole(a.shape) for a in (lengths, one, key_value, back1, back2)]

    def scratch(count):
        return [
            pltpu.VMEM((width, HD), jnp.bfloat16),
            pltpu.VMEM((width, HD), jnp.bfloat16),
            pltpu.VMEM((block_rows, SPAN * block_rows + TILE), jnp.float32),
            pltpu.VMEM((block_rows, count * HD), jnp.bfloat16),
            pltpu.VMEM((block_rows, count * HD), jnp.bfloat16),
            pltpu.SemaphoreType.DMA((2 * block_rows // TILE,)),
        ]

    attended, query_grad, dk, dv = pl.pallas_call(
        functools.partial(first_kernel, first),
        in_specs=inputs,
        out_specs=[anywhere, anywhere, whole(total), whole(total)],
        out_shape=[out, out, pltpu.HBM(total, jnp.float32), pltpu.HBM(total, jnp.float32)],
        scratch_shapes=scratch(first),
        compiler_params=params,
    )(lengths, one, key_value, back1, back2)
    inputs[1] = whole(two.shape)
    return pl.pallas_call(
        functools.partial(second_kernel, heads - first, first),
        in_specs=inputs + [whole(total), whole(total), anywhere, anywhere],
        out_specs=[anywhere, anywhere, whole(pair), whole(pair), whole(pair)],
        out_shape=[
            out, out,
            jax.ShapeDtypeStruct(pair, jnp.float32),
            jax.ShapeDtypeStruct(pair, jnp.bfloat16),
            jax.ShapeDtypeStruct(pair, jnp.bfloat16),
        ],
        scratch_shapes=scratch(heads - first)
        + [pltpu.VMEM(total, jnp.float32), pltpu.VMEM(total, jnp.float32)],
        input_output_aliases={7: 0, 8: 1},
        compiler_params=params,
    )(lengths, two, key_value, back1, back2, *in_hbm(dk, dv), attended, query_grad)


def shifted(block, axis, distance):
    devices = range(lax.axis_size(axis))
    route = [(i - distance, i) for i in devices if i - distance in devices]
    return lax.ppermute(block, axis, route)


def exchange(block):
    moved = lax.all_to_all(block, ("tp", "dp"), split_axis=0, concat_axis=0, tiled=True)
    return moved.reshape(moved.shape[0] * moved.shape[1], moved.shape[2])


def on_device(queries, key_rows, values_in, out_grad, send_rows, doc_lengths):
    replicas, slots = lax.axis_size("dp"), lax.axis_size("tp")
    heads = queries.shape[2] // slots // HD
    key_value = pack_small(send_rows[0], key_rows[0], values_in[0], replicas, slots)
    one, two = pack_large(send_rows[0], queries[0], out_grad[0], replicas, slots, FIRST_HEADS)
    key_value = exchange(key_value)
    previous = [shifted(key_value, "ctx", offset) for offset in range(1, SPAN + 1)]
    one = exchange(one)
    one, two, previous = lax.optimization_barrier((one, two, previous))
    two = exchange(two)
    attended, query_grad, own, back1, back2 = attend(
        one, two, key_value, previous[0], previous[1], doc_lengths, heads, FIRST_HEADS
    )
    for offset, part in ((2, back2), (1, back1)):
        own = own + shifted(part, "ctx", -offset).astype(jnp.float32)
    own = own.astype(jnp.bfloat16)
    return (attended[None], query_grad[None], own[None, :, :HD], own[None, :, HD:])


def solution(mesh):
    rows = P("dp", ("ctx", "tp"), None)
    out = P("dp", "ctx", "tp")
    return jax.shard_map(
        on_device,
        mesh=mesh,
        in_specs=(rows, rows, rows, rows, rows, P("dp", None)),
        out_specs=(out, out, out, out),
        check_vma=False,
    )
```

```python
import functools
import math

import jax
import jax.numpy as jnp
from jax import lax
from jax.experimental import pallas as pl
from jax.experimental.pallas import tpu as pltpu
from jax.sharding import PartitionSpec as P

HD = 128
SPAN = 2
FRONT_HEADS = 4
BACK_HEADS = 4
PACK_SLOTS = 2
TILE = 256
SCALE = 1.0 / math.sqrt(HD)
LOG2_SCALE = math.log2(math.e) * SCALE
NT = (((1,), (1,)), ((), ()))
NN = (((1,), (0,)), ((), ()))
TN = (((0,), (0,)), ((), ()))


def dot(a, b, dims):
    return lax.dot_general(a, b, dims, preferred_element_type=jnp.float32)


def select(order_ref):
    rows = order_ref.shape[1]
    row = lax.broadcasted_iota(jnp.int32, (rows, rows), 0)
    return (row == order_ref[...]).astype(jnp.bfloat16)


def put(ref, slot, begin, moved):
    group = ref.shape[1]
    replicas = moved.shape[0] // group
    for replica in range(replicas):
        ref[slot * replicas + replica, :, begin : begin + moved.shape[1]] = moved[
            replica * group : (replica + 1) * group
        ]


def pack_small_kernel(order_ref, k_ref, v_ref, sent_ref):
    pick = select(order_ref)
    for begin, ref in ((0, k_ref), (HD, v_ref)):
        moved = dot(pick, ref[...], TN).astype(jnp.bfloat16)
        for slot in range(moved.shape[1] // HD):
            put(sent_ref, slot, begin, moved[:, slot * HD : (slot + 1) * HD])


def pack_large_kernel(order_ref, q_ref, g_ref, sent_ref):
    pick = select(order_ref)
    half = sent_ref.shape[2] // 2
    for index, ref in enumerate((q_ref, g_ref)):
        for slot in range(ref.shape[1] // half):
            moved = dot(pick, ref[:, slot * half : (slot + 1) * half], TN)
            put(sent_ref, slot, index * half, moved.astype(jnp.bfloat16))


def in_hbm(*arrays):
    return [pltpu.with_memory_space_constraint(a, pltpu.HBM) for a in arrays]


def pack_small(order, key_rows, values_in, replicas, slots):
    rows, columns = key_rows.shape
    whole = lambda shape: pl.BlockSpec(shape, lambda: (0,) * len(shape))
    sent = (slots * replicas, rows // replicas, 2 * columns // slots)
    return pl.pallas_call(
        pack_small_kernel,
        in_specs=[whole(order.shape), whole(key_rows.shape), whole(values_in.shape)],
        out_specs=whole(sent),
        out_shape=jax.ShapeDtypeStruct(sent, jnp.bfloat16),
        compiler_params=pltpu.CompilerParams(vmem_limit_bytes=16 * 2**20),
    )(*in_hbm(order, key_rows, values_in))


def pack_large(order, queries, out_grad, replicas, slots):
    rows, columns = queries.shape
    half = columns // slots
    wide = pl.BlockSpec((rows, PACK_SLOTS * half), lambda t: (0, t))
    sent = (slots * replicas, rows // replicas, 2 * half)
    return pl.pallas_call(
        pack_large_kernel,
        grid=(slots // PACK_SLOTS,),
        in_specs=[pl.BlockSpec(order.shape, lambda t: (0, 0)), wide, wide],
        out_specs=pl.BlockSpec((PACK_SLOTS * replicas,) + sent[1:], lambda t: (t, 0, 0)),
        out_shape=jax.ShapeDtypeStruct(sent, jnp.bfloat16),
        compiler_params=pltpu.CompilerParams(vmem_limit_bytes=32 * 2**20),
    )(*in_hbm(order, queries, out_grad))


def begin_kernel(lengths_ref, begin_ref):
    block_rows = begin_ref.shape[0]
    docs = lengths_ref.shape[1]
    lengths = lengths_ref[...].astype(jnp.float32)
    down = lax.broadcasted_iota(jnp.int32, (docs, docs), 0)
    across = lax.broadcasted_iota(jnp.int32, (docs, docs), 1)
    column = jnp.sum(jnp.where(down == across, lengths, 0.0), axis=1, keepdims=True)
    starts = jnp.sum(jnp.where(down < across, column, 0.0), axis=0, keepdims=True)
    first = lax.axis_index("ctx") * block_rows
    place = first + lax.broadcasted_iota(jnp.int32, (block_rows, docs), 0)
    begun = starts <= place.astype(jnp.float32)
    begin = jnp.max(jnp.where(begun, starts, 0.0), axis=1, keepdims=True).astype(jnp.int32)
    begin_ref[...] = jnp.broadcast_to(begin - (first - SPAN * block_rows), begin_ref.shape)


def mask(begin, margin, width):
    rows = begin.shape[0]
    row = lax.broadcasted_iota(jnp.int32, (rows, width), 0)
    col = lax.broadcasted_iota(jnp.int32, (rows, width), 1)
    return jnp.where((col <= row + margin) & (col >= begin), 0.0, -1e30)


def stacked(ref, here, begin, heads):
    return jnp.concatenate(
        [ref[here, begin + h * HD : begin + (h + 1) * HD] for h in range(heads)], axis=0
    )


def gather_window(kv_ref, kv1_ref, kv2_ref, key_win, value_win):
    block_rows = kv_ref.shape[0]
    for place, ref in ((0, kv2_ref), (1, kv1_ref), (2, kv_ref)):
        here = slice(place * block_rows, (place + 1) * block_rows)
        key_win[here, :] = ref[:, :HD]
        value_win[here, :HD] = ref[:, HD:]


def front_kernel(
    heads, begin_ref, rows_ref, kv_ref, kv1_ref, kv2_ref,
    prob_ref, dscore_ref, back1_ref, back2_ref,
    key_win, value_win, dk_ref, dv_ref, bias_ref,
):
    gather_window(kv_ref, kv1_ref, kv2_ref, key_win, value_win)
    dk_ref[...] = jnp.zeros_like(dk_ref)
    dv_ref[...] = jnp.zeros_like(dv_ref)
    block_rows = rows_ref.shape[0]
    margin = SPAN * block_rows
    width = margin + TILE
    for head in range(0, heads, FRONT_HEADS):
        for t in range(block_rows // TILE):
            here = slice(t * TILE, (t + 1) * TILE)
            window = slice(t * TILE, t * TILE + width)
            query = stacked(rows_ref, here, head * HD, FRONT_HEADS)
            grad = stacked(rows_ref, here, (heads + head) * HD, FRONT_HEADS)
            scores = dot(query, key_win[window, :], NT)
            if head == 0:
                bias_ref[here, :] = mask(begin_ref[here, :1] - t * TILE, margin, width)
            scores = (scores * LOG2_SCALE).reshape(FRONT_HEADS, TILE, width)
            scores = (scores + bias_ref[here, :][None]).reshape(FRONT_HEADS * TILE, width)
            top = jnp.max(scores, axis=1, keepdims=True)
            expo = jnp.exp2(scores - top)
            inverse = 1.0 / jnp.sum(expo, axis=1, keepdims=True)
            prob = expo.astype(jnp.bfloat16)
            dprob = dot(grad, value_win[window, :], NT)
            delta = jnp.sum(expo * dprob, axis=1, keepdims=True) * inverse
            dscore = (expo * (dprob - delta)).astype(jnp.bfloat16)
            query = (query.astype(jnp.float32) * inverse).astype(jnp.bfloat16)
            grad = (grad.astype(jnp.float32) * inverse).astype(jnp.bfloat16)
            for h in range(FRONT_HEADS):
                part = slice(h * TILE, (h + 1) * TILE)
                prob_ref[head + h, here, :] = prob[part]
                dscore_ref[head + h, here, :] = dscore[part]
            before = margin - t * TILE
            past = slice(t * TILE, margin)
            dv_ref[:, past] += dot(grad, prob[:, :before], TN)
            dk_ref[:, past] += dot(query, dscore[:, :before], TN)
    for place, ref in ((0, back2_ref), (1, back1_ref)):
        here = slice(place * block_rows, (place + 1) * block_rows)
        ref[:, :HD] = (dk_ref[:, here] * SCALE).T.astype(ref.dtype)
        ref[:, HD:] = dv_ref[:, here].T.astype(ref.dtype)


def back_kernel(
    heads, rows_ref, kv_ref, kv1_ref, kv2_ref, prob_ref, dscore_ref,
    out_ref, dq_ref, own_ref,
    key_win, value_win, dk_ref, dv_ref,
):
    gather_window(kv_ref, kv1_ref, kv2_ref, key_win, value_win)
    value_win[:, HD:] = jnp.ones_like(value_win[:, HD:])
    dk_ref[...] = jnp.zeros_like(dk_ref)
    dv_ref[...] = jnp.zeros_like(dv_ref)
    block_rows = rows_ref.shape[0]
    margin = SPAN * block_rows
    width = margin + TILE
    for head in range(0, heads, BACK_HEADS):
        for t in range(block_rows // TILE):
            here = slice(t * TILE, (t + 1) * TILE)
            window = slice(t * TILE, t * TILE + width)
            group = lambda ref: jnp.concatenate(
                [ref[head + h, here, :] for h in range(BACK_HEADS)], axis=0
            )
            prob, dscore = group(prob_ref), group(dscore_ref)
            both = dot(prob, value_win[window, :], NN)
            inverse = 1.0 / both[:, HD:]
            output = (both[:, :HD] * inverse).astype(jnp.bfloat16)
            dquery = dot(dscore, key_win[window, :], NN) * (inverse * SCALE)
            dquery = dquery.astype(jnp.bfloat16)
            for h in range(BACK_HEADS):
                cols = slice((head + h) * HD, (head + h + 1) * HD)
                out_ref[here, cols] = output[h * TILE : (h + 1) * TILE]
                dq_ref[here, cols] = dquery[h * TILE : (h + 1) * TILE]
            query = stacked(rows_ref, here, head * HD, BACK_HEADS)
            grad = stacked(rows_ref, here, (heads + head) * HD, BACK_HEADS)
            query = (query.astype(jnp.float32) * inverse).astype(jnp.bfloat16)
            grad = (grad.astype(jnp.float32) * inverse).astype(jnp.bfloat16)
            before = margin - t * TILE
            reach = slice(0, (t + 1) * TILE)
            dv_ref[:, reach] += dot(grad, prob[:, before:], TN)
            dk_ref[:, reach] += dot(query, dscore[:, before:], TN)
    own_ref[:, :HD] = (dk_ref[...] * SCALE).T
    own_ref[:, HD:] = dv_ref[...].T


def attend(rows, key_value, kv1, kv2, begin, heads):
    block_rows = rows.shape[0]
    margin = SPAN * block_rows
    width = margin + TILE
    pair = key_value.shape
    vmem = pl.BlockSpec(memory_space=pltpu.VMEM)
    whole = lambda shape: pl.BlockSpec(shape, lambda: (0,) * len(shape))
    out = jax.ShapeDtypeStruct((block_rows, heads * HD), jnp.bfloat16)
    sent = jax.ShapeDtypeStruct(pair, jnp.bfloat16)
    work = heads * block_rows * width * HD
    weights = pltpu.VMEM((heads, block_rows, width), jnp.bfloat16)
    inputs = [rows, key_value, kv1, kv2]
    specs = [whole(a.shape) for a in inputs]

    def scratch(value_columns, columns):
        return [
            pltpu.VMEM((margin + block_rows, HD), jnp.bfloat16),
            pltpu.VMEM((margin + block_rows, value_columns), jnp.bfloat16),
            pltpu.VMEM((HD, columns), jnp.float32),
            pltpu.VMEM((HD, columns), jnp.float32),
        ]

    prob, dscore, back1, back2 = pl.pallas_call(
        functools.partial(front_kernel, heads),
        in_specs=[whole(begin.shape)] + specs,
        out_specs=[vmem, vmem, whole(pair), whole(pair)],
        out_shape=[weights, weights, sent, sent],
        scratch_shapes=scratch(HD, margin)
        + [pltpu.VMEM((block_rows, width), jnp.float32)],
        compiler_params=pltpu.CompilerParams(vmem_limit_bytes=25 * 2**20),
        cost_estimate=pl.CostEstimate(
            flops=7 * work, bytes_accessed=8 * work // HD, transcendentals=work // HD
        ),
    )(begin, *inputs)
    attended, query_grad, own = pl.pallas_call(
        functools.partial(back_kernel, heads),
        in_specs=specs + [vmem, vmem],
        out_specs=[whole(out.shape), whole(out.shape), whole(pair)],
        out_shape=[out, out, jax.ShapeDtypeStruct(pair, jnp.float32)],
        scratch_shapes=scratch(2 * HD, block_rows),
        compiler_params=pltpu.CompilerParams(vmem_limit_bytes=18 * 2**20),
        cost_estimate=pl.CostEstimate(
            flops=5 * work, bytes_accessed=8 * work // HD, transcendentals=0
        ),
    )(*inputs, prob, dscore)
    return attended, query_grad, own, back1, back2


def document_begins(lengths, block_rows):
    return pl.pallas_call(
        begin_kernel,
        in_specs=[pl.BlockSpec(lengths.shape, lambda: (0, 0))],
        out_specs=pl.BlockSpec(memory_space=pltpu.VMEM),
        out_shape=pltpu.VMEM((block_rows, HD), jnp.int32),
        compiler_params=pltpu.CompilerParams(vmem_limit_bytes=8 * 2**20),
    )(*in_hbm(lengths))


def shifted(block, axis, distance):
    devices = range(lax.axis_size(axis))
    route = [(i - distance, i) for i in devices if i - distance in devices]
    return lax.ppermute(block, axis, route)


def exchange(block):
    moved = lax.all_to_all(block, ("tp", "dp"), split_axis=0, concat_axis=0, tiled=True)
    return moved.reshape(moved.shape[0] * moved.shape[1], moved.shape[2])


def on_device(queries, key_rows, values_in, out_grad, send_rows, doc_lengths):
    replicas, slots = lax.axis_size("dp"), lax.axis_size("tp")
    heads = queries.shape[2] // slots // HD
    key_value = pack_small(send_rows[0], key_rows[0], values_in[0], replicas, slots)
    rows = pack_large(send_rows[0], queries[0], out_grad[0], replicas, slots)
    key_value = exchange(key_value)
    previous = [shifted(key_value, "ctx", offset) for offset in range(1, SPAN + 1)]
    block_rows = key_value.shape[0]
    lengths, key_value = lax.optimization_barrier((doc_lengths, key_value))
    begin = document_begins(lengths, block_rows)
    rows = exchange(rows)
    attended, query_grad, own, back1, back2 = attend(
        rows, key_value, previous[0], previous[1], begin, heads
    )
    for offset, part in ((2, back2), (1, back1)):
        own = own + shifted(part, "ctx", -offset).astype(jnp.float32)
    own = own.astype(jnp.bfloat16)
    return (attended[None], query_grad[None], own[None, :, :HD], own[None, :, HD:])


def solution(mesh):
    rows = P("dp", ("ctx", "tp"), None)
    out = P("dp", "ctx", "tp")
    return jax.shard_map(
        on_device,
        mesh=mesh,
        in_specs=(rows, rows, rows, rows, rows, P("dp", None)),
        out_specs=(out, out, out, out),
        check_vma=False,
    )
```

```python
import functools
import math

import jax
import jax.numpy as jnp
from jax import lax
from jax.experimental import pallas as pl
from jax.experimental.pallas import tpu as pltpu
from jax.sharding import PartitionSpec as P

HD = 128
SPAN = 2
BACK_HEADS = 4
PACK_SLOTS = 2
TILE = 256
SCALE = 1.0 / math.sqrt(HD)
LOG2_SCALE = math.log2(math.e) * SCALE
NT = (((1,), (1,)), ((), ()))
NN = (((1,), (0,)), ((), ()))
TN = (((0,), (0,)), ((), ()))


def dot(a, b, dims):
    return lax.dot_general(a, b, dims, preferred_element_type=jnp.float32)


def select(order_ref):
    rows = order_ref.shape[1]
    row = lax.broadcasted_iota(jnp.int32, (rows, rows), 0)
    return (row == order_ref[...]).astype(jnp.bfloat16)


def put(ref, slot, begin, moved):
    group = ref.shape[1]
    replicas = moved.shape[0] // group
    for replica in range(replicas):
        ref[slot * replicas + replica, :, begin : begin + moved.shape[1]] = moved[
            replica * group : (replica + 1) * group
        ]


def pack_small_kernel(order_ref, k_ref, v_ref, sent_ref):
    pick = select(order_ref)
    for begin, ref in ((0, k_ref), (HD, v_ref)):
        moved = dot(pick, ref[...], TN).astype(jnp.bfloat16)
        for slot in range(moved.shape[1] // HD):
            put(sent_ref, slot, begin, moved[:, slot * HD : (slot + 1) * HD])


def pack_large_kernel(order_ref, q_ref, g_ref, sent_ref):
    pick = select(order_ref)
    half = sent_ref.shape[2] // 2
    for index, ref in enumerate((q_ref, g_ref)):
        for slot in range(ref.shape[1] // half):
            moved = dot(pick, ref[:, slot * half : (slot + 1) * half], TN)
            put(sent_ref, slot, index * half, moved.astype(jnp.bfloat16))


def in_hbm(*arrays):
    return [pltpu.with_memory_space_constraint(a, pltpu.HBM) for a in arrays]


def pack_small(order, key_rows, values_in, replicas, slots):
    rows, columns = key_rows.shape
    whole = lambda shape: pl.BlockSpec(shape, lambda: (0,) * len(shape))
    sent = (slots * replicas, rows // replicas, 2 * columns // slots)
    return pl.pallas_call(
        pack_small_kernel,
        in_specs=[whole(order.shape), whole(key_rows.shape), whole(values_in.shape)],
        out_specs=whole(sent),
        out_shape=jax.ShapeDtypeStruct(sent, jnp.bfloat16),
        compiler_params=pltpu.CompilerParams(vmem_limit_bytes=16 * 2**20),
    )(*in_hbm(order, key_rows, values_in))


def pack_large(order, queries, out_grad, replicas, slots):
    rows, columns = queries.shape
    half = columns // slots
    wide = pl.BlockSpec((rows, PACK_SLOTS * half), lambda t: (0, t))
    sent = (slots * replicas, rows // replicas, 2 * half)
    return pl.pallas_call(
        pack_large_kernel,
        grid=(slots // PACK_SLOTS,),
        in_specs=[pl.BlockSpec(order.shape, lambda t: (0, 0)), wide, wide],
        out_specs=pl.BlockSpec((PACK_SLOTS * replicas,) + sent[1:], lambda t: (t, 0, 0)),
        out_shape=jax.ShapeDtypeStruct(sent, jnp.bfloat16),
        compiler_params=pltpu.CompilerParams(vmem_limit_bytes=32 * 2**20),
    )(*in_hbm(order, queries, out_grad))


def begin_kernel(lengths_ref, begin_ref):
    block_rows = begin_ref.shape[0]
    docs = lengths_ref.shape[1]
    lengths = lengths_ref[...].astype(jnp.float32)
    down = lax.broadcasted_iota(jnp.int32, (docs, docs), 0)
    across = lax.broadcasted_iota(jnp.int32, (docs, docs), 1)
    column = jnp.sum(jnp.where(down == across, lengths, 0.0), axis=1, keepdims=True)
    starts = jnp.sum(jnp.where(down < across, column, 0.0), axis=0, keepdims=True)
    first = lax.axis_index("ctx") * block_rows
    place = first + lax.broadcasted_iota(jnp.int32, (block_rows, docs), 0)
    begun = starts <= place.astype(jnp.float32)
    begin = jnp.max(jnp.where(begun, starts, 0.0), axis=1, keepdims=True).astype(jnp.int32)
    begin_ref[...] = jnp.broadcast_to(begin - (first - SPAN * block_rows), begin_ref.shape)


def mask(begin, margin, width):
    rows = begin.shape[0]
    row = lax.broadcasted_iota(jnp.int32, (rows, width), 0)
    col = lax.broadcasted_iota(jnp.int32, (rows, width), 1)
    return jnp.where((col <= row + margin) & (col >= begin), 0.0, -1e30)


def stacked(ref, here, begin, heads):
    return jnp.concatenate(
        [ref[here, begin + h * HD : begin + (h + 1) * HD] for h in range(heads)], axis=0
    )


def gather_window(kv_ref, kv1_ref, kv2_ref, key_win, value_win):
    block_rows = kv_ref.shape[0]
    for place, ref in ((0, kv2_ref), (1, kv1_ref), (2, kv_ref)):
        here = slice(place * block_rows, (place + 1) * block_rows)
        key_win[here, :] = ref[:, :HD]
        value_win[here, :HD] = ref[:, HD:]


def front_kernel(
    heads, begin_ref, rows_ref, kv_ref, kv1_ref, kv2_ref,
    prob_ref, dscore_ref, back1_ref, back2_ref,
    key_win, value_win, dk_ref, dv_ref, bias_ref,
):
    gather_window(kv_ref, kv1_ref, kv2_ref, key_win, value_win)
    dk_ref[...] = jnp.zeros_like(dk_ref)
    dv_ref[...] = jnp.zeros_like(dv_ref)
    block_rows = rows_ref.shape[0]
    margin = SPAN * block_rows
    width = margin + TILE
    units = [(head, t) for head in range(heads) for t in range(block_rows // TILE)]

    def spans(t):
        return slice(t * TILE, (t + 1) * TILE), slice(t * TILE, t * TILE + width)

    def columns(head):
        return slice(head * HD, (head + 1) * HD)

    def masked_scores(head, t):
        here, window = spans(t)
        scores = dot(rows_ref[here, columns(head)], key_win[window, :], NT)
        if head == 0:
            bias_ref[here, :] = mask(begin_ref[here, :1] - t * TILE, margin, width)
        scores = scores * LOG2_SCALE + bias_ref[here, :]
        return scores, jnp.max(scores, axis=1, keepdims=True)

    coming = masked_scores(*units[0])
    for index, (head, t) in enumerate(units):
        here, window = spans(t)
        scores, top = coming
        query = rows_ref[here, columns(head)]
        grad = rows_ref[here, columns(heads + head)]
        dprob = dot(grad, value_win[window, :], NT)
        if index + 1 < len(units):
            coming = masked_scores(*units[index + 1])
        expo = jnp.exp2(scores - top)
        inverse = 1.0 / jnp.sum(expo, axis=1, keepdims=True)
        prob = expo.astype(jnp.bfloat16)
        delta = jnp.sum(expo * dprob, axis=1, keepdims=True) * inverse
        dscore = (expo * (dprob - delta)).astype(jnp.bfloat16)
        prob_ref[head, here, :] = prob
        dscore_ref[head, here, :] = dscore
        query = (query.astype(jnp.float32) * inverse).astype(jnp.bfloat16)
        grad = (grad.astype(jnp.float32) * inverse).astype(jnp.bfloat16)
        before = margin - t * TILE
        past = slice(t * TILE, margin)
        dv_ref[:, past] += dot(grad, prob[:, :before], TN)
        dk_ref[:, past] += dot(query, dscore[:, :before], TN)
    for place, ref in ((0, back2_ref), (1, back1_ref)):
        here = slice(place * block_rows, (place + 1) * block_rows)
        ref[:, :HD] = (dk_ref[:, here] * SCALE).T.astype(ref.dtype)
        ref[:, HD:] = dv_ref[:, here].T.astype(ref.dtype)


def back_kernel(
    heads, rows_ref, kv_ref, kv1_ref, kv2_ref, prob_ref, dscore_ref,
    out_ref, dq_ref, own_ref,
    key_win, value_win, dk_ref, dv_ref,
):
    gather_window(kv_ref, kv1_ref, kv2_ref, key_win, value_win)
    value_win[:, HD:] = jnp.ones_like(value_win[:, HD:])
    dk_ref[...] = jnp.zeros_like(dk_ref)
    dv_ref[...] = jnp.zeros_like(dv_ref)
    block_rows = rows_ref.shape[0]
    margin = SPAN * block_rows
    width = margin + TILE
    for head in range(0, heads, BACK_HEADS):
        for t in range(block_rows // TILE):
            here = slice(t * TILE, (t + 1) * TILE)
            window = slice(t * TILE, t * TILE + width)
            group = lambda ref: jnp.concatenate(
                [ref[head + h, here, :] for h in range(BACK_HEADS)], axis=0
            )
            prob, dscore = group(prob_ref), group(dscore_ref)
            both = dot(prob, value_win[window, :], NN)
            inverse = 1.0 / both[:, HD:]
            output = (both[:, :HD] * inverse).astype(jnp.bfloat16)
            dquery = dot(dscore, key_win[window, :], NN) * (inverse * SCALE)
            dquery = dquery.astype(jnp.bfloat16)
            for h in range(BACK_HEADS):
                cols = slice((head + h) * HD, (head + h + 1) * HD)
                out_ref[here, cols] = output[h * TILE : (h + 1) * TILE]
                dq_ref[here, cols] = dquery[h * TILE : (h + 1) * TILE]
            query = stacked(rows_ref, here, head * HD, BACK_HEADS)
            grad = stacked(rows_ref, here, (heads + head) * HD, BACK_HEADS)
            query = (query.astype(jnp.float32) * inverse).astype(jnp.bfloat16)
            grad = (grad.astype(jnp.float32) * inverse).astype(jnp.bfloat16)
            before = margin - t * TILE
            reach = slice(0, (t + 1) * TILE)
            dv_ref[:, reach] += dot(grad, prob[:, before:], TN)
            dk_ref[:, reach] += dot(query, dscore[:, before:], TN)
    own_ref[:, :HD] = (dk_ref[...] * SCALE).T
    own_ref[:, HD:] = dv_ref[...].T


def attend(rows, key_value, kv1, kv2, begin, heads):
    block_rows = rows.shape[0]
    margin = SPAN * block_rows
    width = margin + TILE
    pair = key_value.shape
    vmem = pl.BlockSpec(memory_space=pltpu.VMEM)
    whole = lambda shape: pl.BlockSpec(shape, lambda: (0,) * len(shape))
    out = jax.ShapeDtypeStruct((block_rows, heads * HD), jnp.bfloat16)
    sent = jax.ShapeDtypeStruct(pair, jnp.bfloat16)
    work = heads * block_rows * width * HD
    weights = pltpu.VMEM((heads, block_rows, width), jnp.bfloat16)
    inputs = [rows, key_value, kv1, kv2]
    specs = [whole(a.shape) for a in inputs]

    def scratch(value_columns, columns):
        return [
            pltpu.VMEM((margin + block_rows, HD), jnp.bfloat16),
            pltpu.VMEM((margin + block_rows, value_columns), jnp.bfloat16),
            pltpu.VMEM((HD, columns), jnp.float32),
            pltpu.VMEM((HD, columns), jnp.float32),
        ]

    prob, dscore, back1, back2 = pl.pallas_call(
        functools.partial(front_kernel, heads),
        in_specs=[whole(begin.shape)] + specs,
        out_specs=[vmem, vmem, whole(pair), whole(pair)],
        out_shape=[weights, weights, sent, sent],
        scratch_shapes=scratch(HD, margin)
        + [pltpu.VMEM((block_rows, width), jnp.float32)],
        compiler_params=pltpu.CompilerParams(vmem_limit_bytes=25 * 2**20),
        cost_estimate=pl.CostEstimate(
            flops=7 * work, bytes_accessed=8 * work // HD, transcendentals=work // HD
        ),
    )(begin, *inputs)
    attended, query_grad, own = pl.pallas_call(
        functools.partial(back_kernel, heads),
        in_specs=specs + [vmem, vmem],
        out_specs=[whole(out.shape), whole(out.shape), whole(pair)],
        out_shape=[out, out, jax.ShapeDtypeStruct(pair, jnp.float32)],
        scratch_shapes=scratch(2 * HD, block_rows),
        compiler_params=pltpu.CompilerParams(vmem_limit_bytes=18 * 2**20),
        cost_estimate=pl.CostEstimate(
            flops=5 * work, bytes_accessed=8 * work // HD, transcendentals=0
        ),
    )(*inputs, prob, dscore)
    return attended, query_grad, own, back1, back2


def document_begins(lengths, block_rows):
    return pl.pallas_call(
        begin_kernel,
        in_specs=[pl.BlockSpec(lengths.shape, lambda: (0, 0))],
        out_specs=pl.BlockSpec(memory_space=pltpu.VMEM),
        out_shape=pltpu.VMEM((block_rows, HD), jnp.int32),
        compiler_params=pltpu.CompilerParams(vmem_limit_bytes=8 * 2**20),
    )(*in_hbm(lengths))


def shifted(block, axis, distance):
    devices = range(lax.axis_size(axis))
    route = [(i - distance, i) for i in devices if i - distance in devices]
    return lax.ppermute(block, axis, route)


def exchange(block):
    moved = lax.all_to_all(block, ("tp", "dp"), split_axis=0, concat_axis=0, tiled=True)
    return moved.reshape(moved.shape[0] * moved.shape[1], moved.shape[2])


def on_device(queries, key_rows, values_in, out_grad, send_rows, doc_lengths):
    replicas, slots = lax.axis_size("dp"), lax.axis_size("tp")
    heads = queries.shape[2] // slots // HD
    key_value = pack_small(send_rows[0], key_rows[0], values_in[0], replicas, slots)
    rows = pack_large(send_rows[0], queries[0], out_grad[0], replicas, slots)
    key_value = exchange(key_value)
    previous = [shifted(key_value, "ctx", offset) for offset in range(1, SPAN + 1)]
    block_rows = key_value.shape[0]
    lengths, key_value = lax.optimization_barrier((doc_lengths, key_value))
    begin = document_begins(lengths, block_rows)
    rows = exchange(rows)
    attended, query_grad, own, back1, back2 = attend(
        rows, key_value, previous[0], previous[1], begin, heads
    )
    two, one = shifted(back2, "ctx", -2), shifted(back1, "ctx", -1)
    key_grad, value_grad = (
        (own[:, c] + two[:, c].astype(jnp.float32) + one[:, c].astype(jnp.float32)).astype(two.dtype)
        for c in (slice(0, HD), slice(HD, 2 * HD))
    )
    return (attended[None], query_grad[None], key_grad[None], value_grad[None])


def solution(mesh):
    rows = P("dp", ("ctx", "tp"), None)
    out = P("dp", "ctx", "tp")
    return jax.shard_map(
        on_device,
        mesh=mesh,
        in_specs=(rows, rows, rows, rows, rows, P("dp", None)),
        out_specs=(out, out, out, out),
        check_vma=False,
    )
```

```python
import functools
import math

import jax
import jax.numpy as jnp
from jax import lax
from jax.experimental import pallas as pl
from jax.experimental.pallas import tpu as pltpu
from jax.sharding import PartitionSpec as P

HD = 128
SPAN = 2
BACK_HEADS = 4
PACK_SLOTS = 2
TILE = 256
SCALE = 1.0 / math.sqrt(HD)
LOG2_SCALE = math.log2(math.e) * SCALE
NT = (((1,), (1,)), ((), ()))
NN = (((1,), (0,)), ((), ()))
TN = (((0,), (0,)), ((), ()))


def dot(a, b, dims):
    return lax.dot_general(a, b, dims, preferred_element_type=jnp.float32)


def select(order_ref):
    rows = order_ref.shape[1]
    row = lax.broadcasted_iota(jnp.int32, (rows, rows), 0)
    return (row == order_ref[...]).astype(jnp.bfloat16)


def put(ref, slot, begin, moved):
    group = ref.shape[1]
    replicas = moved.shape[0] // group
    for replica in range(replicas):
        ref[slot * replicas + replica, :, begin : begin + moved.shape[1]] = moved[
            replica * group : (replica + 1) * group
        ]


def pack_small_kernel(order_ref, k_ref, v_ref, sent_ref):
    pick = select(order_ref)
    for begin, ref in ((0, k_ref), (HD, v_ref)):
        moved = dot(pick, ref[...], TN).astype(jnp.bfloat16)
        for slot in range(moved.shape[1] // HD):
            put(sent_ref, slot, begin, moved[:, slot * HD : (slot + 1) * HD])


def pack_large_kernel(order_ref, q_ref, g_ref, sent_ref):
    pick = select(order_ref)
    half = sent_ref.shape[2] // 2
    for index, ref in enumerate((q_ref, g_ref)):
        for slot in range(ref.shape[1] // half):
            moved = dot(pick, ref[:, slot * half : (slot + 1) * half], TN)
            put(sent_ref, slot, index * half, moved.astype(jnp.bfloat16))


def in_hbm(*arrays):
    return [pltpu.with_memory_space_constraint(a, pltpu.HBM) for a in arrays]


def pack_small(order, key_rows, values_in, replicas, slots):
    rows, columns = key_rows.shape
    whole = lambda shape: pl.BlockSpec(shape, lambda: (0,) * len(shape))
    sent = (slots * replicas, rows // replicas, 2 * columns // slots)
    return pl.pallas_call(
        pack_small_kernel,
        in_specs=[whole(order.shape), whole(key_rows.shape), whole(values_in.shape)],
        out_specs=whole(sent),
        out_shape=jax.ShapeDtypeStruct(sent, jnp.bfloat16),
        compiler_params=pltpu.CompilerParams(vmem_limit_bytes=16 * 2**20),
    )(*in_hbm(order, key_rows, values_in))


def pack_large(order, queries, out_grad, replicas, slots):
    rows, columns = queries.shape
    half = columns // slots
    wide = pl.BlockSpec((rows, PACK_SLOTS * half), lambda t: (0, t))
    sent = (slots * replicas, rows // replicas, 2 * half)
    return pl.pallas_call(
        pack_large_kernel,
        grid=(slots // PACK_SLOTS,),
        in_specs=[pl.BlockSpec(order.shape, lambda t: (0, 0)), wide, wide],
        out_specs=pl.BlockSpec((PACK_SLOTS * replicas,) + sent[1:], lambda t: (t, 0, 0)),
        out_shape=jax.ShapeDtypeStruct(sent, jnp.bfloat16),
        compiler_params=pltpu.CompilerParams(vmem_limit_bytes=32 * 2**20),
    )(*in_hbm(order, queries, out_grad))


def begin_kernel(lengths_ref, begin_ref):
    block_rows = begin_ref.shape[0]
    docs = lengths_ref.shape[1]
    lengths = lengths_ref[...].astype(jnp.float32)
    down = lax.broadcasted_iota(jnp.int32, (docs, docs), 0)
    across = lax.broadcasted_iota(jnp.int32, (docs, docs), 1)
    column = jnp.sum(jnp.where(down == across, lengths, 0.0), axis=1, keepdims=True)
    starts = jnp.sum(jnp.where(down < across, column, 0.0), axis=0, keepdims=True)
    first = lax.axis_index("ctx") * block_rows
    place = first + lax.broadcasted_iota(jnp.int32, (block_rows, docs), 0)
    begun = starts <= place.astype(jnp.float32)
    begin = jnp.max(jnp.where(begun, starts, 0.0), axis=1, keepdims=True).astype(jnp.int32)
    begin_ref[...] = jnp.broadcast_to(begin - (first - SPAN * block_rows), begin_ref.shape)


def mask(begin, margin, width):
    rows = begin.shape[0]
    row = lax.broadcasted_iota(jnp.int32, (rows, width), 0)
    col = lax.broadcasted_iota(jnp.int32, (rows, width), 1)
    return jnp.where((col <= row + margin) & (col >= begin), 0.0, -1e30)


def stacked(ref, here, begin, heads):
    return jnp.concatenate(
        [ref[here, begin + h * HD : begin + (h + 1) * HD] for h in range(heads)], axis=0
    )


def gather_window(kv_ref, kv1_ref, kv2_ref, key_win, value_win):
    block_rows = kv_ref.shape[0]
    for place, ref in ((0, kv2_ref), (1, kv1_ref), (2, kv_ref)):
        here = slice(place * block_rows, (place + 1) * block_rows)
        key_win[here, :] = ref[:, :HD]
        value_win[here, :HD] = ref[:, HD:]


def front_kernel(
    heads, begin_ref, rows_ref, kv_ref, kv1_ref, kv2_ref,
    prob_ref, dscore_ref, back1_ref, back2_ref,
    key_win, value_win, dk_ref, dv_ref, bias_ref,
):
    gather_window(kv_ref, kv1_ref, kv2_ref, key_win, value_win)
    dk_ref[...] = jnp.zeros_like(dk_ref)
    dv_ref[...] = jnp.zeros_like(dv_ref)
    block_rows = rows_ref.shape[0]
    margin = SPAN * block_rows
    width = margin + TILE
    units = [(head, t) for head in range(heads) for t in range(block_rows // TILE)]

    def spans(t):
        return slice(t * TILE, (t + 1) * TILE), slice(t * TILE, t * TILE + width)

    def columns(head):
        return slice(head * HD, (head + 1) * HD)

    def masked_scores(head, t):
        here, window = spans(t)
        scores = dot(rows_ref[here, columns(head)], key_win[window, :], NT)
        if head == 0:
            bias_ref[here, :] = mask(begin_ref[here, :1] - t * TILE, margin, width)
        scores = scores * LOG2_SCALE + bias_ref[here, :]
        return scores, jnp.max(scores, axis=1, keepdims=True)

    coming = masked_scores(*units[0])
    for index, (head, t) in enumerate(units):
        here, window = spans(t)
        scores, top = coming
        query = rows_ref[here, columns(head)]
        grad = rows_ref[here, columns(heads + head)]
        dprob = dot(grad, value_win[window, :], NT)
        if index + 1 < len(units):
            coming = masked_scores(*units[index + 1])
        expo = jnp.exp2(scores - top)
        inverse = 1.0 / jnp.sum(expo, axis=1, keepdims=True)
        prob = expo.astype(jnp.bfloat16)
        delta = jnp.sum(expo * dprob, axis=1, keepdims=True) * inverse
        dscore = (expo * (dprob - delta)).astype(jnp.bfloat16)
        prob_ref[head, here, :] = prob
        dscore_ref[head, here, :] = dscore
        query = (query.astype(jnp.float32) * inverse).astype(jnp.bfloat16)
        grad = (grad.astype(jnp.float32) * inverse).astype(jnp.bfloat16)
        before = margin - t * TILE
        past = slice(t * TILE, margin)
        dv_ref[:, past] += dot(grad, prob[:, :before], TN)
        dk_ref[:, past] += dot(query, dscore[:, :before], TN)
    for place, ref in ((0, back2_ref), (1, back1_ref)):
        here = slice(place * block_rows, (place + 1) * block_rows)
        ref[:, :HD] = (dk_ref[:, here] * SCALE).T.astype(ref.dtype)
        ref[:, HD:] = dv_ref[:, here].T.astype(ref.dtype)


def back_kernel(
    heads, rows_ref, kv_ref, kv1_ref, kv2_ref, prob_ref, dscore_ref,
    out_ref, dq_ref, own_ref,
    key_win, value_win, dk_ref, dv_ref,
):
    gather_window(kv_ref, kv1_ref, kv2_ref, key_win, value_win)
    value_win[:, HD:] = jnp.ones_like(value_win[:, HD:])
    dk_ref[...] = jnp.zeros_like(dk_ref)
    dv_ref[...] = jnp.zeros_like(dv_ref)
    block_rows = rows_ref.shape[0]
    margin = SPAN * block_rows
    width = margin + TILE
    for head in range(0, heads, BACK_HEADS):
        for t in range(block_rows // TILE):
            here = slice(t * TILE, (t + 1) * TILE)
            window = slice(t * TILE, t * TILE + width)
            group = lambda ref: jnp.concatenate(
                [ref[head + h, here, :] for h in range(BACK_HEADS)], axis=0
            )
            prob, dscore = group(prob_ref), group(dscore_ref)
            both = dot(prob, value_win[window, :], NN)
            inverse = 1.0 / both[:, HD:]
            output = (both[:, :HD] * inverse).astype(jnp.bfloat16)
            dquery = dot(dscore, key_win[window, :], NN) * (inverse * SCALE)
            dquery = dquery.astype(jnp.bfloat16)
            for h in range(BACK_HEADS):
                cols = slice((head + h) * HD, (head + h + 1) * HD)
                out_ref[here, cols] = output[h * TILE : (h + 1) * TILE]
                dq_ref[here, cols] = dquery[h * TILE : (h + 1) * TILE]
            query = stacked(rows_ref, here, head * HD, BACK_HEADS)
            grad = stacked(rows_ref, here, (heads + head) * HD, BACK_HEADS)
            query = (query.astype(jnp.float32) * inverse).astype(jnp.bfloat16)
            grad = (grad.astype(jnp.float32) * inverse).astype(jnp.bfloat16)
            before = margin - t * TILE
            reach = slice(0, (t + 1) * TILE)
            dv_ref[:, reach] += dot(grad, prob[:, before:], TN)
            dk_ref[:, reach] += dot(query, dscore[:, before:], TN)
    own_ref[:, :HD] = (dk_ref[...] * SCALE).T
    own_ref[:, HD:] = dv_ref[...].T


def attend(rows, key_value, kv1, kv2, begin, heads):
    block_rows = rows.shape[0]
    margin = SPAN * block_rows
    width = margin + TILE
    pair = key_value.shape
    vmem = pl.BlockSpec(memory_space=pltpu.VMEM)
    whole = lambda shape: pl.BlockSpec(shape, lambda: (0,) * len(shape))
    out = jax.ShapeDtypeStruct((block_rows, heads * HD), jnp.bfloat16)
    sent = jax.ShapeDtypeStruct(pair, jnp.bfloat16)
    work = heads * block_rows * width * HD
    weights = pltpu.VMEM((heads, block_rows, width), jnp.bfloat16)
    inputs = [rows, key_value, kv1, kv2]
    specs = [whole(a.shape) for a in inputs]

    def scratch(value_columns, columns):
        return [
            pltpu.VMEM((margin + block_rows, HD), jnp.bfloat16),
            pltpu.VMEM((margin + block_rows, value_columns), jnp.bfloat16),
            pltpu.VMEM((HD, columns), jnp.float32),
            pltpu.VMEM((HD, columns), jnp.float32),
        ]

    prob, dscore, back1, back2 = pl.pallas_call(
        functools.partial(front_kernel, heads),
        in_specs=[whole(begin.shape)] + specs,
        out_specs=[vmem, vmem, whole(pair), whole(pair)],
        out_shape=[weights, weights, sent, sent],
        scratch_shapes=scratch(HD, margin)
        + [pltpu.VMEM((block_rows, width), jnp.float32)],
        compiler_params=pltpu.CompilerParams(vmem_limit_bytes=25 * 2**20),
        cost_estimate=pl.CostEstimate(
            flops=7 * work, bytes_accessed=8 * work // HD, transcendentals=work // HD
        ),
    )(begin, *inputs)
    attended, query_grad, own = pl.pallas_call(
        functools.partial(back_kernel, heads),
        in_specs=specs + [vmem, vmem],
        out_specs=[whole(out.shape), whole(out.shape), whole(pair)],
        out_shape=[out, out, jax.ShapeDtypeStruct(pair, jnp.float32)],
        scratch_shapes=scratch(2 * HD, block_rows),
        compiler_params=pltpu.CompilerParams(vmem_limit_bytes=18 * 2**20),
        cost_estimate=pl.CostEstimate(
            flops=5 * work, bytes_accessed=8 * work // HD, transcendentals=0
        ),
    )(*inputs, prob, dscore)
    return attended, query_grad, own, back1, back2


def document_begins(lengths, block_rows):
    return pl.pallas_call(
        begin_kernel,
        in_specs=[pl.BlockSpec(lengths.shape, lambda: (0, 0))],
        out_specs=pl.BlockSpec(memory_space=pltpu.VMEM),
        out_shape=pltpu.VMEM((block_rows, HD), jnp.int32),
        compiler_params=pltpu.CompilerParams(vmem_limit_bytes=8 * 2**20),
    )(*in_hbm(lengths))


def shifted(block, axis, distance):
    devices = range(lax.axis_size(axis))
    route = [(i - distance, i) for i in devices if i - distance in devices]
    return lax.ppermute(block, axis, route)


def exchange(block):
    moved = lax.all_to_all(block, ("tp", "dp"), split_axis=0, concat_axis=0, tiled=True)
    return moved.reshape(moved.shape[0] * moved.shape[1], moved.shape[2])


def on_device(queries, key_rows, values_in, out_grad, send_rows, doc_lengths):
    replicas, slots = lax.axis_size("dp"), lax.axis_size("tp")
    heads = queries.shape[2] // slots // HD
    key_value = pack_small(send_rows[0], key_rows[0], values_in[0], replicas, slots)
    rows = pack_large(send_rows[0], queries[0], out_grad[0], replicas, slots)
    key_value = exchange(key_value)
    previous = [shifted(key_value, "ctx", offset) for offset in range(1, SPAN + 1)]
    block_rows = key_value.shape[0]
    lengths, key_value = lax.optimization_barrier((doc_lengths, key_value))
    begin = document_begins(lengths, block_rows)
    rows = exchange(rows)
    attended, query_grad, own, back1, back2 = attend(
        rows, key_value, previous[0], previous[1], begin, heads
    )
    one, two = shifted(back1, "ctx", -1), shifted(back2, "ctx", -2)
    key_grad, value_grad = (
        (own[:, c] + one[:, c].astype(jnp.float32) + two[:, c].astype(jnp.float32)).astype(one.dtype)
        for c in (slice(0, HD), slice(HD, 2 * HD))
    )
    return (attended[None], query_grad[None], key_grad[None], value_grad[None])


def solution(mesh):
    rows = P("dp", ("ctx", "tp"), None)
    out = P("dp", "ctx", "tp")
    return jax.shard_map(
        on_device,
        mesh=mesh,
        in_specs=(rows, rows, rows, rows, rows, P("dp", None)),
        out_specs=(out, out, out, out),
        check_vma=False,
    )
```
